32 devices in a mesh: row: 4 (over y, core), col: 8 (over z, x).
Axes of the slice: x: 2, y: 2, z: 4, core: 2. Of those that a mesh axis runs over, the one named last changes fastest.
Arguments:
- blocks: bfloat16 [1536, 16, 4096], P('col', 'row'), may hold values from -1.75 to 1.75
- columns: int32 [1536, 16], P('col', 'row'), may hold values from 0 to 383, as said below
- counts: int32 [1536, 4], P('col', 'row'), may hold values from 0 to 4, as said below
Outputs:
- product: bfloat16 [1536, 16, 4096], P('col', 'row')
The draws below stay inside these ranges and needn't reach their ends.
Inputs may be any that keep to these rules, and one draw needn't show every extreme that they name: `counts`: in each tile, every block row has between 0 and 4 live slots; in every tile some block row has exactly 4. The live slots of a block row name different tile columns, at most 2 of them below 192 and at most 2 at or above; in every tile some block row reaches 2 in both halves. A live tile column t of global block row g satisfies (t - g) mod 192 < 8. Dead slots hold arbitrary values in the range.
All inputs are finite; a program needn't handle non-finite values.
Results may differ from the reference program's by a relative error of at most 0.001.
Values may be sent and summed in bfloat16 or wider, within the bound.
A program may use at most 192 MiB of HBM per device.

```python
import jax
import jax.numpy as jnp
from jax import lax

BLK = 64
HS = 2
BAND = 8
SECTIONS = 2
SLOTS = 4
NB = 1536
WB = 192
BB = 4096
N_ROW = 4
N_COL = 8


def pattern(key):
    keys = jax.random.split(jax.random.fold_in(key, 7), 9)
    first_count = jax.random.randint(keys[0], (NB, N_ROW), 0, HS + 1)
    second_count = jax.random.randint(keys[1], (NB, N_ROW), 0, HS + 1)
    pick = jax.random.randint(keys[2], (NB // WB, N_ROW), 0, WB)
    strip_pos = (jnp.arange(NB, dtype=jnp.int32) % WB)[:, None]
    filled = strip_pos == jnp.repeat(pick, WB, axis=0)
    first_count = jnp.where(filled, HS, first_count)
    second_count = jnp.where(filled, HS, second_count)
    global_row = jnp.arange(NB, dtype=jnp.int32)[:, None, None]
    member = jnp.arange(HS, dtype=jnp.int32)[None, None, :]
    first_base = jax.random.randint(keys[3], (NB, N_ROW, 1), 0, BAND)
    first_step = 2 * jax.random.randint(keys[4], (NB, N_ROW, 1), 0, BAND // 2) + 1
    second_base = jax.random.randint(keys[5], (NB, N_ROW, 1), 0, BAND)
    second_step = 2 * jax.random.randint(keys[6], (NB, N_ROW, 1), 0, BAND // 2) + 1
    first_cols = (global_row + (first_base + member * first_step) % BAND) % WB
    second_cols = WB + (global_row + (second_base + member * second_step) % BAND) % WB
    slot_ids = jnp.arange(SLOTS, dtype=jnp.int32)[None, None, :]
    fc = first_count[:, :, None]
    sc = second_count[:, :, None]
    first_take = jnp.take_along_axis(first_cols, jnp.clip(slot_ids, 0, HS - 1) * jnp.ones_like(fc), axis=2)
    second_take = jnp.take_along_axis(second_cols, jnp.clip(slot_ids - fc, 0, HS - 1), axis=2)
    garbage = jax.random.randint(keys[7], (NB, N_ROW, SLOTS), 0, 2 * WB)
    listed = jnp.where(slot_ids < fc, first_take, jnp.where(slot_ids < fc + sc, second_take, garbage))
    total = first_count + second_count
    scores = jax.random.randint(keys[8], (NB, N_ROW, SLOTS), 0, 2 ** 20) * 8 + slot_ids
    scores = jnp.where(slot_ids < total[:, :, None], scores, 2 ** 28 + slot_ids)
    order = jnp.argsort(scores, axis=-1, stable=True)
    listed = jnp.take_along_axis(listed, order, axis=-1)
    return (listed.reshape(NB, N_ROW * SLOTS).astype(jnp.int32), total.astype(jnp.int32))


def draw_columns(key, part):
    return pattern(key)[0]


def draw_counts(key, part):
    return pattern(key)[1]


def steps_of(key, dims, pieces, low, top_value):
    def one(dim, blocks):
        draws = jax.random.uniform(jax.random.fold_in(jax.random.fold_in(key, 6), dim), (blocks,), jnp.float32, low / len(pieces), top_value / len(pieces))
        return jnp.repeat(jnp.exp(draws), dims[dim] // blocks).reshape((-1,) + (1,) * (len(dims) - dim - 1))

    loudness = one(*pieces[0])
    for cut in pieces[1:]:
        loudness = loudness * one(*cut)
    return loudness


def centred(rng, extent, deviation, bound, cuts=(), held_as=jnp.bfloat16):
    values = deviation * jax.random.normal(rng, extent, jnp.float32)
    if cuts:
        values = values * steps_of(rng, extent, cuts, -0.22, 0.18)
    return jnp.clip(values, -bound, bound).astype(held_as)


def setup_inputs(seed: int = 0) -> dict:
    streams_of = jax.random.split(jax.random.key(seed), 4)
    return {
        "blocks": centred(streams_of[0], (NB, N_ROW * SLOTS, BB), 0.3, 1.75, ((0, 8), (1, 4))),
        "columns": draw_columns(jax.random.fold_in(streams_of[3], 71), 0),
        "counts": draw_counts(jax.random.fold_in(streams_of[3], 71), 0),
    }


def compact(tile_blocks, tile_cols, tile_count, half_index):
    strip_count = tile_cols.shape[0]
    slot_count = tile_cols.shape[1]
    slot_ids = jnp.arange(slot_count, dtype=jnp.int32)
    live_slots = (slot_ids[None, :] < tile_count[:, None]) & (tile_cols // strip_count == half_index)
    position = jnp.cumsum(live_slots.astype(jnp.int32), axis=1) - 1
    chosen = live_slots[:, :, None] & (position[:, :, None] == jnp.arange(HS, dtype=jnp.int32)[None, None, :])
    picked = jnp.einsum('isq,isx->iqx', chosen.astype(jnp.float32), tile_blocks.astype(jnp.float32)).astype(jnp.bfloat16)
    inner_rows = jnp.sum(jnp.where(chosen, (tile_cols - half_index * strip_count)[:, :, None], 0), axis=1).astype(jnp.int32)
    used_flags = jnp.any(chosen, axis=1).astype(jnp.int32)
    return picked, inner_rows, used_flags


def section_term(picked, inner_rows, used_flags, right_blocks, right_cols, right_count, out_cols, out_live):
    strip_count = picked.shape[0]
    slot_count = out_cols.shape[1]
    gathered = right_blocks[inner_rows]
    gathered_cols = right_cols[inner_rows]
    gathered_count = right_count[inner_rows]
    slot_ids = jnp.arange(slot_count, dtype=jnp.int32)
    right_live = slot_ids[None, None, :] < gathered_count[:, :, None]
    matches = (gathered_cols[:, :, :, None] == out_cols[:, None, None, :]) & right_live[:, :, :, None]
    matches = matches & (used_flags[:, :, None, None] > 0) & out_live[:, None, None, :]
    selected = jnp.einsum('iqbj,iqbx->iqjx', matches.astype(jnp.float32), gathered.astype(jnp.float32)).astype(jnp.bfloat16)
    left_blocks = picked.reshape(strip_count, HS, BLK, BLK).astype(jnp.float32)
    right_sel = selected.reshape(strip_count, HS, slot_count, BLK, BLK).astype(jnp.float32)
    contribution = jnp.einsum('iqmn,iqjnp->ijmp', left_blocks, right_sel)
    return contribution.reshape(strip_count, slot_count, BLK * BLK)


def reference(blocks, columns, counts):
    def take(piece, owner):
        start_row = (piece * WB).astype(jnp.int32)
        start_slot = (owner * SLOTS).astype(jnp.int32)
        zero_index = jnp.int32(0)
        tile_blocks = lax.dynamic_slice(blocks, (start_row, start_slot, zero_index), (WB, SLOTS, BB))
        tile_cols = lax.dynamic_slice(columns, (start_row, start_slot), (WB, SLOTS))
        tile_count = lax.dynamic_slice(counts, (start_row, owner.astype(jnp.int32)), (WB, 1))[:, 0]
        return tile_blocks, tile_cols, tile_count

    def one_device(device):
        col_id = (device // N_ROW).astype(jnp.int32)
        row_id = (device % N_ROW).astype(jnp.int32)
        own_blocks, own_cols, own_count = take(col_id, row_id)
        out_live = jnp.arange(SLOTS, dtype=jnp.int32)[None, :] < own_count[:, None]
        accumulated = jnp.zeros((WB, SLOTS, BB), jnp.float32)
        for section in range(SECTIONS):
            target_piece = ((col_id + section) % N_COL).astype(jnp.int32)
            root_index = (target_piece // 2).astype(jnp.int32)
            half_index = (target_piece % 2).astype(jnp.int32)
            left_tile = take(col_id, root_index)
            picked, inner_rows, used_flags = compact(left_tile[0], left_tile[1], left_tile[2], half_index)
            right_tile = take(target_piece, row_id)
            accumulated = accumulated + section_term(picked, inner_rows, used_flags, right_tile[0], right_tile[1], right_tile[2], own_cols, out_live)
        return accumulated.astype(jnp.bfloat16)

    tiles = lax.map(one_device, jnp.arange(N_COL * N_ROW, dtype=jnp.int32))
    tiles = tiles.reshape(N_COL, N_ROW, WB, SLOTS, BB).transpose(0, 2, 1, 3, 4)
    return tiles.reshape(NB, N_ROW * SLOTS, BB)
```

```python
import functools

import jax
import jax.numpy as jnp
from jax import lax
from jax.experimental import pallas as pl
from jax.experimental.pallas import tpu as pltpu
from jax.sharding import PartitionSpec as P

BLK = 64
HS = 2
BAND = 8
SECTIONS = 2
CAP = 160
SHIFT = 1024
VMEM_LIMIT = 50 * 1024 * 1024
MESH = pl.DeviceIdType.MESH


def broadcast(block, axis, owner):
    block = jnp.where(lax.axis_index(axis) == owner, block, jnp.zeros_like(block))
    return lax.psum(block, axis)


def from_behind(block, axis, distance):
    devices = range(lax.axis_size(axis))
    route = [((i - distance) % len(devices), i) for i in devices]
    return lax.ppermute(block, axis, route)


def compact(tile_blocks, tile_cols, tile_count, half_index):
    strip_count = tile_cols.shape[0]
    slot_count = tile_cols.shape[1]
    slot_ids = jnp.arange(slot_count, dtype=jnp.int32)
    live_slots = (slot_ids[None, :] < tile_count[:, None]) & (
        tile_cols // strip_count == half_index
    )
    position = jnp.cumsum(live_slots.astype(jnp.int32), axis=1) - 1
    chosen = live_slots[:, :, None] & (
        position[:, :, None] == jnp.arange(HS, dtype=jnp.int32)[None, None, :]
    )
    picked = jnp.einsum(
        "isq,isx->iqx",
        chosen.astype(jnp.bfloat16),
        tile_blocks,
        preferred_element_type=jnp.bfloat16,
    )
    inner_rows = jnp.sum(
        jnp.where(chosen, (tile_cols - half_index * strip_count)[:, :, None], 0), axis=1
    ).astype(jnp.int32)
    used_flags = jnp.any(chosen, axis=1).astype(jnp.int32)
    return (picked, inner_rows, used_flags)


def section_term(
    picked, inner_rows, used_flags, right_blocks, right_cols, right_count, out_cols, out_live
):
    strip_count = picked.shape[0]
    slot_count = out_cols.shape[1]
    gathered = right_blocks[inner_rows]
    gathered_cols = right_cols[inner_rows]
    gathered_count = right_count[inner_rows]
    slot_ids = jnp.arange(slot_count, dtype=jnp.int32)
    right_live = slot_ids[None, None, :] < gathered_count[:, :, None]
    matches = (gathered_cols[:, :, :, None] == out_cols[:, None, None, :]) & right_live[
        :, :, :, None
    ]
    matches = matches & (used_flags[:, :, None, None] > 0) & out_live[:, None, None, :]
    selected = jnp.einsum(
        "iqbj,iqbx->iqjx",
        matches.astype(jnp.bfloat16),
        gathered,
        preferred_element_type=jnp.bfloat16,
    )
    left_blocks = picked.reshape(strip_count, HS, BLK, BLK)
    right_sel = selected.reshape(strip_count, HS, slot_count, BLK, BLK)
    contribution = jnp.einsum(
        "iqmn,iqjnp->ijmp", left_blocks, right_sel, preferred_element_type=jnp.float32
    )
    return contribution.reshape(strip_count, slot_count, BLK * BLK)


def dense_local(blocks, columns, counts):
    count_now = counts[:, 0]
    strip_count = columns.shape[0]
    slot_count = columns.shape[1]
    out_live = jnp.arange(slot_count, dtype=jnp.int32)[None, :] < count_now[:, None]
    col_index = lax.axis_index("col")
    col_total = lax.axis_size("col")
    accumulated = jnp.zeros((strip_count, slot_count, blocks.shape[2]), jnp.float32)
    right_tile = (blocks, columns, count_now)
    for section in range(SECTIONS):
        target_piece = (col_index + section) % col_total
        root_index = target_piece // 2
        half_index = target_piece % 2
        got_blocks, got_cols, got_count = (
            broadcast(blocks, "row", root_index),
            broadcast(columns, "row", root_index),
            broadcast(count_now, "row", root_index),
        )
        picked, inner_rows, used_flags = compact(got_blocks, got_cols, got_count, half_index)
        if section > 0:
            right_tile = from_behind((right_tile[0], right_tile[1], right_tile[2]), "col", -1)
        accumulated = accumulated + section_term(
            picked,
            inner_rows,
            used_flags,
            right_tile[0],
            right_tile[1],
            right_tile[2],
            columns,
            out_live,
        )
    return accumulated.astype(jnp.bfloat16)


def match(left, half, right, out):
    rows = left.shape[2]
    slots = left.shape[1]
    row = jnp.arange(rows, dtype=jnp.int32)
    inner = jnp.full_like(left, 0)
    reach = jnp.full((left.shape[0], slots, slots, rows), -2, jnp.int32)
    for step in range(BAND):
        there = (row + step) % rows
        hit = left == half[:, None, None] * rows + there
        inner = jnp.where(hit, there, inner)
        moved = jnp.roll(right, -step, axis=2)
        reach = jnp.where(hit[:, :, None], moved[:, None], reach)
    found = jnp.zeros((left.shape[0], slots, slots, rows), jnp.bool_)
    which = jnp.zeros((left.shape[0], slots, slots, rows), jnp.int32)
    live = (out >= 0)[:, None]
    for b in range(slots):
        same = (reach[:, :, b][:, :, None] == out[:, None]) & live
        found = found | same
        which = jnp.where(same, b, which)
    slot = jnp.arange(slots, dtype=jnp.int32)
    code = row * slots + slot[:, None, None]
    code = code + SHIFT * (inner[:, :, None] * slots + which)
    code = code + SHIFT * SHIFT * slot[:, None]
    lists = left.shape[0]
    return found.reshape(lists, slots * slots, rows), code.reshape(lists, slots * slots, rows)


def packed_lists(found, code):
    ones = found.astype(jnp.bfloat16)
    rows = found.shape[2]
    combos = found.shape[1]
    before_row = jnp.triu(jnp.ones((rows, rows), jnp.bfloat16), 1)
    before_combo = jnp.tril(jnp.ones((combos, combos), jnp.bfloat16), -1)
    per_row = jnp.sum(found.astype(jnp.int32), axis=1).astype(jnp.bfloat16)
    base = jnp.dot(per_row, before_row, preferred_element_type=jnp.float32)
    inside = jnp.einsum("cd,ldr->lcr", before_combo, ones, preferred_element_type=jnp.float32)
    place = (base[:, None, :] + inside).astype(jnp.int32)
    place = jnp.where(found, place, -1)
    rank = jnp.arange(CAP, dtype=jnp.int32)
    taken = place[:, None] == rank[None, :, None, None]
    return jnp.sum(jnp.where(taken, code[:, None], 0), axis=(2, 3))


def gather_kernel(n_row, lists, counts, tile, r_self, r_send, l_send):
    me = lax.axis_index("row")
    col = lax.axis_index("col")
    n_col = lax.axis_size("col")

    def pick(count, which, dst, divide):
        def one(k, carry):
            index = lax.rem(lists[which, k] // divide, SHIFT)
            dst[k] = tile[index]
            return carry

        lax.fori_loop(0, count, one, 0)

    pick(counts[me], me, r_self, SHIFT)
    pick(counts[2 * n_row], 2 * n_row, r_send, SHIFT)
    for section in range(SECTIONS):
        owner = lax.rem(col + section, n_col) // 2

        @pl.when(owner == me)
        def _():
            def one(q, carry):
                which = section * n_row + q
                pick(counts[which], which, l_send.at[section, q], 1)
                return carry

            lax.fori_loop(0, n_row, one, 0)


def exchange_kernel(n_row, n_col, r_send, l_send, r_recv, l_recv, rs, rr, ls, lr):
    me = lax.axis_index("row")
    col = lax.axis_index("col")
    ahead, behind = lax.rem(col + 1, n_col), lax.rem(col + n_col - 1, n_col)
    barrier = pltpu.get_barrier_semaphore()
    pl.semaphore_signal(barrier, inc=1, device_id=(me, ahead), device_id_type=MESH)
    pl.semaphore_signal(barrier, inc=1, device_id=(me, behind), device_id_type=MESH)
    for step in range(1, n_row):
        peer = lax.rem(me + step, n_row)
        pl.semaphore_signal(barrier, inc=1, device_id=(peer, col), device_id_type=MESH)
    pl.semaphore_wait(barrier, n_row + 1)

    right = pltpu.make_async_remote_copy(
        src_ref=r_send, dst_ref=r_recv, send_sem=rs, recv_sem=rr,
        device_id=(me, behind), device_id_type=MESH,
    )
    right.start()

    def left(section, step):
        peer = lax.rem(me + step, n_row)
        return pltpu.make_async_remote_copy(
            src_ref=l_send.at[section, peer], dst_ref=l_recv.at[section],
            send_sem=ls.at[section, step], recv_sem=lr.at[section],
            device_id=(peer, col), device_id_type=MESH,
        )

    owners = [lax.rem(col + section, n_col) // 2 for section in range(SECTIONS)]
    for section in range(SECTIONS):

        @pl.when(owners[section] == me)
        def _():
            for step in range(1, n_row):
                left(section, step).start()
            own = pltpu.make_async_copy(
                l_send.at[section, me], l_recv.at[section], ls.at[section, 0]
            )
            own.start()
            own.wait()

    for section in range(SECTIONS):

        @pl.when(owners[section] == me)
        def _():
            for step in range(1, n_row):
                left(section, step).wait_send()

        @pl.when(owners[section] != me)
        def _():
            left(section, 1).wait_recv()

    right.wait()


def product_kernel(slots, lists, counts, lefts, r_self, r_recv, out, total, ready):
    rows = out.shape[0]
    deep = BLK // 2
    wide = 2 * BLK
    tiles = BLK * BLK // wide

    def clear(i, carry):
        out[i] = jnp.zeros((slots, BLK * BLK), out.dtype)
        return carry

    lax.fori_loop(0, rows, clear, 0)

    src = lax.broadcasted_iota(jnp.int32, (wide, wide), 0)
    dst = lax.broadcasted_iota(jnp.int32, (wide, wide), 1)
    place = (src // BLK) * BLK + (src % 2) * deep + (src % BLK) // 2
    order = jnp.where(place == dst, 1.0, 0.0).astype(jnp.bfloat16)
    lane = lax.broadcasted_iota(jnp.int32, (deep, wide), 1)

    for section in range(SECTIONS):

        def start(k, carry):
            row = lax.rem(lists[section, k], SHIFT) // slots
            total[pl.ds(row * (slots * deep), slots * deep), :] = jnp.zeros(
                (slots * deep, wide), jnp.float32
            )
            ready[section, k] = jnp.dot(
                lefts[section, k], order, preferred_element_type=jnp.float32
            ).astype(jnp.bfloat16)
            return carry

        lax.fori_loop(0, counts[section], start, 0)

    for section, rights in enumerate((r_self, r_recv)):

        def multiply(k, carry):
            code = lists[section, k]
            row = lax.rem(code, SHIFT) // slots
            slot = code // (SHIFT * SHIFT)
            block = rights[k].astype(jnp.float32)
            turned = pltpu.roll(block, BLK, 1)
            weight = jnp.concatenate(
                [
                    jnp.where(lane < BLK, block, 0.0),
                    jnp.where(lane < BLK, turned, 0.0),
                    jnp.where(lane < BLK, 0.0, turned),
                    jnp.where(lane < BLK, 0.0, block),
                ],
                axis=0,
            ).astype(jnp.bfloat16)
            here = pl.ds((row * slots + slot) * deep, deep)
            total[here, :] += jnp.dot(
                ready[section, k], weight, preferred_element_type=jnp.float32
            )
            return carry

        lax.fori_loop(0, counts[section], multiply, 0)

    for section in range(SECTIONS):

        def finish(k, carry):
            row = lax.rem(lists[section, k], SHIFT) // slots
            for part in range(tiles):
                piece = total[pl.ds(row * (slots * deep) + part, slots, stride=deep), :]
                out[row, :, part * wide : (part + 1) * wide] = piece.astype(out.dtype)
            return carry

        lax.fori_loop(0, counts[section], finish, 0)


def sparse_local(blocks, lists, counts):
    rows, slots, size = blocks.shape
    n_row, n_col = lax.axis_size("row"), lax.axis_size("col")
    me = lax.axis_index("row")
    form = (BLK // 2, 2 * BLK)
    tile = blocks.reshape((rows * slots,) + form)
    smem = pl.BlockSpec(memory_space=pltpu.SMEM)
    vmem = pl.BlockSpec(memory_space=pltpu.VMEM)
    anywhere = pl.BlockSpec(memory_space=pl.ANY)
    one = jax.ShapeDtypeStruct((CAP,) + form, jnp.bfloat16)
    r_self, r_send, l_send = pl.pallas_call(
        functools.partial(gather_kernel, n_row),
        out_shape=(
            one, one, jax.ShapeDtypeStruct((SECTIONS, n_row, CAP) + form, jnp.bfloat16),
        ),
        in_specs=[smem, smem, vmem],
        out_specs=(vmem, vmem, vmem),
        compiler_params=pltpu.CompilerParams(vmem_limit_bytes=VMEM_LIMIT),
        name="pick_blocks",
    )(lists, counts, tile)
    r_recv, l_recv = pl.pallas_call(
        functools.partial(exchange_kernel, n_row, n_col),
        out_shape=(one, jax.ShapeDtypeStruct((SECTIONS, CAP) + form, jnp.bfloat16)),
        in_specs=[anywhere, anywhere],
        out_specs=(anywhere, anywhere),
        scratch_shapes=[
            pltpu.SemaphoreType.DMA,
            pltpu.SemaphoreType.DMA,
            pltpu.SemaphoreType.DMA((SECTIONS, n_row)),
            pltpu.SemaphoreType.DMA((SECTIONS,)),
        ],
        compiler_params=pltpu.CompilerParams(collective_id=0, has_side_effects=True),
        name="exchange_blocks",
    )(r_send, l_send)
    mine = jnp.stack([me, n_row + me])
    return pl.pallas_call(
        functools.partial(product_kernel, slots),
        out_shape=jax.ShapeDtypeStruct(blocks.shape, jnp.bfloat16),
        in_specs=[smem, smem, vmem, vmem, vmem],
        out_specs=vmem,
        scratch_shapes=[
            pltpu.VMEM((rows * slots * form[0], form[1]), jnp.float32),
            pltpu.VMEM((SECTIONS, CAP) + form, jnp.bfloat16),
        ],
        compiler_params=pltpu.CompilerParams(vmem_limit_bytes=VMEM_LIMIT),
        name="multiply_blocks",
    )(lists[mine], counts[mine], l_recv, r_self, r_recv)


def local(blocks, columns, counts):
    rows, slots = columns.shape
    n_row, n_col = lax.axis_size("row"), lax.axis_size("col")
    me, col = lax.axis_index("row"), lax.axis_index("col")
    slot_ids = jnp.arange(slots, dtype=jnp.int32)
    live = jnp.where(slot_ids[None, :] < counts, columns, -1).T
    every = lax.all_gather(live, ("col", "row")).reshape(n_col, n_row, slots, rows)

    pieces = [[(c + s) % n_col for s in range(SECTIONS)] for c in range(n_col)]
    lefts = jnp.stack([every[c, m // 2] for c in range(n_col) for m in pieces[c]])
    lefts = jnp.repeat(lefts, n_row, axis=0)
    halves = jnp.array([m % 2 for c in range(n_col) for m in pieces[c]], jnp.int32)
    halves = jnp.repeat(halves, n_row)
    rights = jnp.stack([jnp.roll(every, -s, axis=0) for s in range(SECTIONS)], axis=1)
    outs = jnp.stack([every] * SECTIONS, axis=1)
    flat = (n_col * SECTIONS * n_row, slots, rows)
    found, _ = match(lefts, halves, rights.reshape(flat), outs.reshape(flat))
    longest = jnp.max(jnp.sum(found.astype(jnp.int32), axis=(1, 2)))

    behind = lax.rem(col + n_col - 1, n_col)
    group = SECTIONS * n_row

    def ours(array):
        array = array.reshape((n_col, group) + array.shape[1:])
        first = lax.dynamic_index_in_dim(array, col, 0, keepdims=False)
        last = lax.dynamic_index_in_dim(array, behind, 0, keepdims=False)
        last = lax.dynamic_slice_in_dim(last, n_row + me, 1, 0)
        return jnp.concatenate([first, last])

    found, code = match(
        ours(lefts), ours(halves), ours(rights.reshape(flat)), ours(outs.reshape(flat))
    )
    sizes = jnp.sum(found.astype(jnp.int32), axis=(1, 2))
    lists = packed_lists(found, code)
    return lax.cond(
        longest <= CAP,
        lambda: sparse_local(blocks, lists, sizes),
        lambda: dense_local(blocks, columns, counts),
    )


def solution(mesh):
    return jax.shard_map(
        local,
        mesh=mesh,
        in_specs=(P("col", "row", None), P("col", "row"), P("col", "row")),
        out_specs=P("col", "row", None),
        check_vma=False,
    )
```

```python
import functools

import jax
import jax.numpy as jnp
from jax import lax
from jax.experimental import pallas as pl
from jax.experimental.pallas import tpu as pltpu
from jax.sharding import PartitionSpec as P

BLK = 64
HS = 2
BAND = 8
SECTIONS = 2
SEND = 128
KEEP = 224
HIGH, LOW = 8, 32
UNROLL = 4
SHIFT = 1024
VMEM_LIMIT = 50 * 1024 * 1024
MESH = pl.DeviceIdType.MESH


def broadcast(block, axis, owner):
    block = jnp.where(lax.axis_index(axis) == owner, block, jnp.zeros_like(block))
    return lax.psum(block, axis)


def from_behind(block, axis, distance):
    devices = range(lax.axis_size(axis))
    route = [((i - distance) % len(devices), i) for i in devices]
    return lax.ppermute(block, axis, route)


def compact(tile_blocks, tile_cols, tile_count, half_index):
    strip_count = tile_cols.shape[0]
    slot_count = tile_cols.shape[1]
    slot_ids = jnp.arange(slot_count, dtype=jnp.int32)
    live_slots = (slot_ids[None, :] < tile_count[:, None]) & (
        tile_cols // strip_count == half_index
    )
    position = jnp.cumsum(live_slots.astype(jnp.int32), axis=1) - 1
    chosen = live_slots[:, :, None] & (
        position[:, :, None] == jnp.arange(HS, dtype=jnp.int32)[None, None, :]
    )
    picked = jnp.einsum(
        "isq,isx->iqx",
        chosen.astype(jnp.bfloat16),
        tile_blocks,
        preferred_element_type=jnp.bfloat16,
    )
    inner_rows = jnp.sum(
        jnp.where(chosen, (tile_cols - half_index * strip_count)[:, :, None], 0), axis=1
    ).astype(jnp.int32)
    used_flags = jnp.any(chosen, axis=1).astype(jnp.int32)
    return (picked, inner_rows, used_flags)


def section_term(
    picked, inner_rows, used_flags, right_blocks, right_cols, right_count, out_cols, out_live
):
    strip_count = picked.shape[0]
    slot_count = out_cols.shape[1]
    gathered = right_blocks[inner_rows]
    gathered_cols = right_cols[inner_rows]
    gathered_count = right_count[inner_rows]
    slot_ids = jnp.arange(slot_count, dtype=jnp.int32)
    right_live = slot_ids[None, None, :] < gathered_count[:, :, None]
    matches = (gathered_cols[:, :, :, None] == out_cols[:, None, None, :]) & right_live[
        :, :, :, None
    ]
    matches = matches & (used_flags[:, :, None, None] > 0) & out_live[:, None, None, :]
    selected = jnp.einsum(
        "iqbj,iqbx->iqjx",
        matches.astype(jnp.bfloat16),
        gathered,
        preferred_element_type=jnp.bfloat16,
    )
    left_blocks = picked.reshape(strip_count, HS, BLK, BLK)
    right_sel = selected.reshape(strip_count, HS, slot_count, BLK, BLK)
    contribution = jnp.einsum(
        "iqmn,iqjnp->ijmp", left_blocks, right_sel, preferred_element_type=jnp.float32
    )
    return contribution.reshape(strip_count, slot_count, BLK * BLK)


def dense_local(blocks, columns, counts):
    count_now = counts[:, 0]
    strip_count = columns.shape[0]
    slot_count = columns.shape[1]
    out_live = jnp.arange(slot_count, dtype=jnp.int32)[None, :] < count_now[:, None]
    col_index = lax.axis_index("col")
    col_total = lax.axis_size("col")
    accumulated = jnp.zeros((strip_count, slot_count, blocks.shape[2]), jnp.float32)
    right_tile = (blocks, columns, count_now)
    for section in range(SECTIONS):
        target_piece = (col_index + section) % col_total
        root_index = target_piece // 2
        half_index = target_piece % 2
        got_blocks, got_cols, got_count = (
            broadcast(blocks, "row", root_index),
            broadcast(columns, "row", root_index),
            broadcast(count_now, "row", root_index),
        )
        picked, inner_rows, used_flags = compact(got_blocks, got_cols, got_count, half_index)
        if section > 0:
            right_tile = from_behind((right_tile[0], right_tile[1], right_tile[2]), "col", -1)
        accumulated = accumulated + section_term(
            picked,
            inner_rows,
            used_flags,
            right_tile[0],
            right_tile[1],
            right_tile[2],
            columns,
            out_live,
        )
    return accumulated.astype(jnp.bfloat16)


def columns_kernel(n_row, n_col, live, every, rs, rr, cs, cr):
    me, col = lax.axis_index("row"), lax.axis_index("col")
    barrier = pltpu.get_barrier_semaphore()

    def row_peer(step):
        return lax.rem(me + step, n_row), col

    def col_peer(step):
        return me, lax.rem(col + step, n_col)

    for step in range(1, n_row):
        pl.semaphore_signal(barrier, inc=1, device_id=row_peer(step), device_id_type=MESH)
    for step in range(1, n_col):
        pl.semaphore_signal(barrier, inc=1, device_id=col_peer(step), device_id_type=MESH)
    every[col * n_row + me] = live[...]
    pl.semaphore_wait(barrier, n_row + n_col - 2)

    def along_row(step, owner):
        return pltpu.make_async_remote_copy(
            src_ref=live, dst_ref=every.at[col * n_row + owner],
            send_sem=rs.at[step], recv_sem=rr.at[step],
            device_id=row_peer(step), device_id_type=MESH,
        )

    def along_col(step, owner):
        return pltpu.make_async_remote_copy(
            src_ref=every.at[pl.ds(col * n_row, n_row)],
            dst_ref=every.at[pl.ds(owner * n_row, n_row)],
            send_sem=cs.at[step], recv_sem=cr.at[step],
            device_id=col_peer(step), device_id_type=MESH,
        )

    for step in range(1, n_row):
        along_row(step, me).start()
    for step in range(1, n_row):
        along_row(step, lax.rem(me + n_row - step, n_row)).wait_recv()
    for step in range(1, n_col):
        along_col(step, col).start()
    for step in range(1, n_row):
        along_row(step, me).wait_send()
    for step in range(1, n_col):
        along_col(step, lax.rem(col + n_col - step, n_col)).wait_recv()
    for step in range(1, n_col):
        along_col(step, col).wait_send()


def match_kernel(n_row, n_col, rows, every, per_row, listed):
    slots, wide = every.shape[1:]
    combos = slots * slots
    me, col = lax.axis_index("row"), lax.axis_index("col")
    lane = lax.broadcasted_iota(jnp.int32, (combos, wide), 1)

    def found_in(c, section, q):
        piece = lax.rem(c + section, n_col)
        left = every[c * n_row + piece // 2]
        right = every[piece * n_row + q]
        out = every[c * n_row + q]
        left = jnp.concatenate(
            [jnp.broadcast_to(left[t : t + 1], (slots, wide)) for t in range(slots)], axis=0
        )
        out = jnp.where(lane < rows, jnp.concatenate([out] * slots, axis=0), -1)
        left = left - lax.rem(piece, 2) * rows
        inner = jnp.zeros((combos, wide), jnp.int32)
        reach = [jnp.full((combos, wide), -2, jnp.int32) for _ in range(slots)]
        for step in range(BAND):
            there = jnp.where(lane + step < rows, lane + step, lane + step - rows)
            hit = left == there
            inner = jnp.where(hit, there, inner)
            moved = right if step == 0 else pltpu.roll(right, wide - step, 1)
            for b in range(slots):
                reach[b] = jnp.where(
                    hit, jnp.broadcast_to(moved[b : b + 1], (combos, wide)), reach[b]
                )
        found = jnp.zeros((combos, wide), jnp.int32)
        which = jnp.zeros((combos, wide), jnp.int32)
        for b in range(slots):
            same = (reach[b] == out) & (out >= 0)
            found = jnp.where(same, 1, found)
            which = jnp.where(same, b, which)
        return found, inner, which

    group = SECTIONS * n_row

    def count(which, carry):
        c = which // group
        rest = which - c * group
        found, _, _ = found_in(c, rest // n_row, lax.rem(rest, n_row))
        per_row[which] = jnp.sum(found, axis=0, keepdims=True)
        return carry

    lax.fori_loop(0, n_col * group, count, 0)

    up_r = lax.broadcasted_iota(jnp.int32, (wide, wide), 0)
    up_c = lax.broadcasted_iota(jnp.int32, (wide, wide), 1)
    before_row = jnp.where(up_r < up_c, 1.0, 0.0).astype(jnp.bfloat16)
    in_r = lax.broadcasted_iota(jnp.int32, (combos, combos), 0)
    in_c = lax.broadcasted_iota(jnp.int32, (combos, combos), 1)
    before_combo = jnp.where(in_c < in_r, 1.0, 0.0).astype(jnp.bfloat16)
    high = lax.broadcasted_iota(jnp.int32, (HIGH, wide), 0)
    low = lax.broadcasted_iota(jnp.int32, (LOW, wide), 0)
    row = lax.broadcasted_iota(jnp.int32, (1, wide), 1).astype(jnp.float32)

    def build(which, carry):
        last = which == group
        c = jnp.where(last, lax.rem(col + n_col - 1, n_col), col)
        section = jnp.where(last, SECTIONS - 1, which // n_row)
        q = jnp.where(last, me, lax.rem(which, n_row))
        found, inner, slot = found_in(c, section, q)
        ones = found.astype(jnp.float32)
        base = jnp.dot(
            jnp.broadcast_to(jnp.sum(ones, axis=0, keepdims=True), (combos, wide)).astype(
                jnp.bfloat16
            ),
            before_row,
            preferred_element_type=jnp.float32,
        )
        inside = jnp.dot(
            before_combo, ones.astype(jnp.bfloat16), preferred_element_type=jnp.float32
        )
        place = jnp.where(found > 0, (base + inside).astype(jnp.int32), -1)
        total = jnp.zeros((3 * HIGH, LOW), jnp.float32)
        for combo in range(combos):
            at = place[combo : combo + 1]
            on = high == at // LOW
            small = (slot[combo : combo + 1] * combos + combo).astype(jnp.float32)
            deep = inner[combo : combo + 1].astype(jnp.float32)
            values = jnp.concatenate(
                [
                    jnp.where(on, jnp.broadcast_to(value, (HIGH, wide)), 0.0)
                    for value in (row, deep, small)
                ],
                axis=0,
            ).astype(jnp.bfloat16)
            keys = jnp.where((low == lax.rem(at, LOW)) & (at >= 0), 1.0, 0.0)
            total += lax.dot_general(
                values,
                keys.astype(jnp.bfloat16),
                (((1,), (1,)), ((), ())),
                preferred_element_type=jnp.float32,
            )
        listed[which] = total.astype(jnp.int32)
        return carry

    lax.fori_loop(0, group + 1, build, 0)


def gather_kernel(n_row, lists, counts, tile, r_self, r_send, l_self, l_send):
    me = lax.axis_index("row")
    col = lax.axis_index("col")
    n_col = lax.axis_size("col")

    def pick(which, dst, divide):
        def some(step, carry):
            for part in range(UNROLL):
                k = step * UNROLL + part
                dst[k] = tile[lax.rem(lists[which, k] // divide, SHIFT)]
            return carry

        lax.fori_loop(0, (counts[which] + UNROLL - 1) // UNROLL, some, 0)

    pick(me, r_self, SHIFT)
    pick(2 * n_row, r_send, SHIFT)
    for section in range(SECTIONS):
        owner = lax.rem(col + section, n_col) // 2

        @pl.when(owner == me)
        def _():
            def one(q, carry):
                pick(section * n_row + q, l_send.at[section, q], 1)
                return carry

            if section == 0:
                pick(me, l_self, 1)
                lax.fori_loop(0, me, one, 0)
                lax.fori_loop(me + 1, n_row, one, 0)
            else:
                lax.fori_loop(0, n_row, one, 0)


def exchange_kernel(
    n_row, n_col, r_send, l_self, l_send, r_recv, l_first, l_next, rs, rr, ls, lr
):
    me = lax.axis_index("row")
    col = lax.axis_index("col")
    ahead, behind = lax.rem(col + 1, n_col), lax.rem(col + n_col - 1, n_col)
    barrier = pltpu.get_barrier_semaphore()
    pl.semaphore_signal(barrier, inc=1, device_id=(me, ahead), device_id_type=MESH)
    pl.semaphore_signal(barrier, inc=1, device_id=(me, behind), device_id_type=MESH)
    for step in range(1, n_row):
        peer = lax.rem(me + step, n_row)
        pl.semaphore_signal(barrier, inc=1, device_id=(peer, col), device_id_type=MESH)
    pl.semaphore_wait(barrier, n_row + 1)

    right = pltpu.make_async_remote_copy(
        src_ref=r_send, dst_ref=r_recv, send_sem=rs, recv_sem=rr,
        device_id=(me, behind), device_id_type=MESH,
    )
    right.start()

    def landing(section):
        return l_first.at[pl.ds(0, SEND)] if section == 0 else l_next

    def left(section, step):
        peer = lax.rem(me + step, n_row)
        return pltpu.make_async_remote_copy(
            src_ref=l_send.at[section, peer], dst_ref=landing(section),
            send_sem=ls.at[section, step], recv_sem=lr.at[section],
            device_id=(peer, col), device_id_type=MESH,
        )

    owners = [lax.rem(col + section, n_col) // 2 for section in range(SECTIONS)]
    for section in range(SECTIONS):

        @pl.when(owners[section] == me)
        def _():
            for step in range(1, n_row):
                left(section, step).start()
            own = pltpu.make_async_copy(
                l_self if section == 0 else l_send.at[section, me],
                l_first if section == 0 else l_next,
                ls.at[section, 0],
            )
            own.start()
            own.wait()

    for section in range(SECTIONS):

        @pl.when(owners[section] == me)
        def _():
            for step in range(1, n_row):
                left(section, step).wait_send()

        @pl.when(owners[section] != me)
        def _():
            left(section, 1).wait_recv()

    right.wait()


def product_kernel(
    slots, lists, counts, l_first, l_next, r_self, r_recv, out, total, first, second, done
):
    rows = out.shape[0]
    deep = BLK // 2
    wide = 2 * BLK
    tiles = BLK * BLK // wide
    spare = rows * slots

    def clear(i, carry):
        out[i] = jnp.zeros((slots, BLK * BLK), out.dtype)
        done[i] = 0
        return carry

    lax.fori_loop(0, rows, clear, 0)

    src = lax.broadcasted_iota(jnp.int32, (wide, wide), 0)
    dst = lax.broadcasted_iota(jnp.int32, (wide, wide), 1)
    place = (src // BLK) * BLK + (src % 2) * deep + (src % BLK) // 2
    order = jnp.where(place == dst, 1.0, 0.0).astype(jnp.bfloat16)
    lane = lax.broadcasted_iota(jnp.int32, (deep, wide), 1)

    for section, (source, ready) in enumerate(((l_first, first), (l_next, second))):
        batch = 8

        def start(step, carry):
            here = pl.ds(step * batch, batch)
            ready[here] = (
                jnp.dot(
                    source[here].reshape(batch * deep, wide),
                    order,
                    preferred_element_type=jnp.float32,
                )
                .astype(jnp.bfloat16)
                .reshape(batch, deep, wide)
            )
            for part in range(batch):
                row = lax.rem(lists[section, step * batch + part], SHIFT) // slots
                total[pl.ds(row * (slots * deep), slots * deep), :] = jnp.zeros(
                    (slots * deep, wide), jnp.float32
                )
            return carry

        lax.fori_loop(0, (counts[section] + batch - 1) // batch, start, 0)

    for section, (ready, rights) in enumerate(((first, r_self), (second, r_recv))):
        count = counts[section]

        def multiply(step, carry):
            found = []
            for part in range(UNROLL):
                k = step * UNROLL + part
                block = rights[k].astype(jnp.float32)
                turned = pltpu.roll(block, BLK, 1)
                weight = jnp.concatenate(
                    [
                        jnp.where(lane < BLK, block, 0.0),
                        jnp.where(lane < BLK, turned, 0.0),
                        jnp.where(lane < BLK, 0.0, turned),
                        jnp.where(lane < BLK, 0.0, block),
                    ],
                    axis=0,
                ).astype(jnp.bfloat16)
                found.append(
                    jnp.dot(ready[k], weight, preferred_element_type=jnp.float32)
                )
            for part in range(UNROLL):
                k = step * UNROLL + part
                code = lists[section, k]
                target = lax.rem(code, SHIFT) // slots * slots + code // (SHIFT * SHIFT)
                target = jnp.where(k < count, target, spare)
                total[pl.ds(target * deep, deep), :] += found[part]
            return carry

        lax.fori_loop(0, (count + UNROLL - 1) // UNROLL, multiply, 0)

    for section in range(SECTIONS):

        def finish(k, carry):
            row = lax.rem(lists[section, k], SHIFT) // slots

            @pl.when(done[row] == 0)
            def _():
                done[row] = 1
                for part in range(tiles):
                    piece = total[pl.ds(row * (slots * deep) + part, slots, stride=deep), :]
                    out[row, :, part * wide : (part + 1) * wide] = piece.astype(out.dtype)

            return carry

        lax.fori_loop(0, counts[section], finish, 0)


def sparse_local(blocks, lists, counts):
    rows, slots, size = blocks.shape
    n_row, n_col = lax.axis_size("row"), lax.axis_size("col")
    me = lax.axis_index("row")
    form = (BLK // 2, 2 * BLK)
    tile = blocks.reshape((rows * slots,) + form)
    smem = pl.BlockSpec(memory_space=pltpu.SMEM)
    vmem = pl.BlockSpec(memory_space=pltpu.VMEM)
    anywhere = pl.BlockSpec(memory_space=pl.ANY)
    kept = jax.ShapeDtypeStruct((KEEP,) + form, jnp.bfloat16)
    sent = jax.ShapeDtypeStruct((SEND,) + form, jnp.bfloat16)
    all_sent = jax.ShapeDtypeStruct((SECTIONS, n_row, SEND) + form, jnp.bfloat16)
    r_self, r_send, l_self, l_send = pl.pallas_call(
        functools.partial(gather_kernel, n_row),
        out_shape=(kept, sent, kept, all_sent),
        in_specs=[smem, smem, vmem],
        out_specs=(vmem, vmem, vmem, vmem),
        compiler_params=pltpu.CompilerParams(vmem_limit_bytes=VMEM_LIMIT),
        name="pick_blocks",
    )(lists, counts, tile)
    r_recv, l_first, l_next = pl.pallas_call(
        functools.partial(exchange_kernel, n_row, n_col),
        out_shape=(sent, kept, sent),
        in_specs=[anywhere] * 3,
        out_specs=(anywhere,) * 3,
        scratch_shapes=[
            pltpu.SemaphoreType.DMA,
            pltpu.SemaphoreType.DMA,
            pltpu.SemaphoreType.DMA((SECTIONS, n_row)),
            pltpu.SemaphoreType.DMA((SECTIONS,)),
        ],
        compiler_params=pltpu.CompilerParams(collective_id=0, has_side_effects=True),
        name="exchange_blocks",
    )(r_send, l_self, l_send)
    mine = jnp.stack([me, n_row + me])
    return pl.pallas_call(
        functools.partial(product_kernel, slots),
        out_shape=jax.ShapeDtypeStruct(blocks.shape, jnp.bfloat16),
        in_specs=[smem, smem] + [vmem] * 4,
        out_specs=vmem,
        scratch_shapes=[
            pltpu.VMEM(((rows * slots + 1) * form[0], form[1]), jnp.float32),
            pltpu.VMEM((KEEP,) + form, jnp.bfloat16),
            pltpu.VMEM((SEND,) + form, jnp.bfloat16),
            pltpu.SMEM((rows,), jnp.int32),
        ],
        compiler_params=pltpu.CompilerParams(vmem_limit_bytes=VMEM_LIMIT),
        name="multiply_blocks",
    )(lists[mine], counts[mine], l_first, l_next, r_self, r_recv)


def local(blocks, columns, counts):
    rows, slots = columns.shape
    n_row, n_col = lax.axis_size("row"), lax.axis_size("col")
    me, col = lax.axis_index("row"), lax.axis_index("col")
    slot_ids = jnp.arange(slots, dtype=jnp.int32)
    live = jnp.where(slot_ids[None, :] < counts, columns, -1).T
    wide = -(-(rows + BAND) // 128) * 128
    fill = jnp.full((slots, wide - rows - BAND), -1, jnp.int32)
    live = jnp.concatenate([live, live[:, :BAND], fill], axis=1)
    vmem = pl.BlockSpec(memory_space=pltpu.VMEM)
    every = pl.pallas_call(
        functools.partial(columns_kernel, n_row, n_col),
        out_shape=jax.ShapeDtypeStruct((n_col * n_row, slots, wide), jnp.int32),
        in_specs=[vmem],
        out_specs=vmem,
        scratch_shapes=[
            pltpu.SemaphoreType.DMA((n_row,)),
            pltpu.SemaphoreType.DMA((n_row,)),
            pltpu.SemaphoreType.DMA((n_col,)),
            pltpu.SemaphoreType.DMA((n_col,)),
        ],
        compiler_params=pltpu.CompilerParams(collective_id=1, has_side_effects=True),
        name="exchange_columns",
    )(live)

    group = SECTIONS * n_row
    per_row, listed = pl.pallas_call(
        functools.partial(match_kernel, n_row, n_col, rows),
        out_shape=(
            jax.ShapeDtypeStruct((n_col * group, 1, wide), jnp.int32),
            jax.ShapeDtypeStruct((group + 1, 3 * HIGH, LOW), jnp.int32),
        ),
        in_specs=[vmem],
        out_specs=(vmem, vmem),
        compiler_params=pltpu.CompilerParams(vmem_limit_bytes=VMEM_LIMIT),
        name="match_columns",
    )(every)
    totals = jnp.sum(per_row, axis=(1, 2)).reshape(n_col, SECTIONS, n_row)
    c = jnp.arange(n_col)[:, None, None]
    s = jnp.arange(SECTIONS)[None, :, None]
    stays = (s == 0) & (jnp.arange(n_row)[None, None, :] == c // 2)
    fits = jnp.all(totals <= jnp.where(stays, KEEP, SEND))

    behind = lax.rem(col + n_col - 1, n_col)
    sizes = jnp.concatenate(
        [
            lax.dynamic_index_in_dim(totals, col, 0, keepdims=False).reshape(group),
            lax.dynamic_slice(totals, (behind, SECTIONS - 1, me), (1, 1, 1)).reshape(1),
        ]
    )
    row, inner, small = [
        listed[:, part * HIGH : (part + 1) * HIGH].reshape(group + 1, HIGH * LOW)
        for part in range(3)
    ]
    slot = small // (slots * slots)
    combo = small % (slots * slots)
    lists = row * slots + combo // slots + SHIFT * (inner * slots + slot)
    lists = lists + SHIFT * SHIFT * (combo % slots)
    return lax.cond(
        fits,
        lambda: sparse_local(blocks, lists, sizes),
        lambda: dense_local(blocks, columns, counts),
    )


def solution(mesh):
    return jax.shard_map(
        local,
        mesh=mesh,
        in_specs=(P("col", "row", None), P("col", "row"), P("col", "row")),
        out_specs=P("col", "row", None),
        check_vma=False,
    )
```

```python
import functools

import jax
import jax.numpy as jnp
from jax import lax
from jax.experimental import pallas as pl
from jax.experimental.pallas import tpu as pltpu
from jax.sharding import PartitionSpec as P

BLK = 64
HS = 2
BAND = 8
SECTIONS = 2
SEND = 96
LEFT = 64
KEEP = 224
HIGH, LOW = 8, 32
UNROLL = 4
SHIFT = 1024
VMEM_LIMIT = 50 * 1024 * 1024
MESH = pl.DeviceIdType.MESH


def broadcast(block, axis, owner):
    block = jnp.where(lax.axis_index(axis) == owner, block, jnp.zeros_like(block))
    return lax.psum(block, axis)


def from_behind(block, axis, distance):
    devices = range(lax.axis_size(axis))
    route = [((i - distance) % len(devices), i) for i in devices]
    return lax.ppermute(block, axis, route)


def compact(tile_blocks, tile_cols, tile_count, half_index):
    strip_count = tile_cols.shape[0]
    slot_count = tile_cols.shape[1]
    slot_ids = jnp.arange(slot_count, dtype=jnp.int32)
    live_slots = (slot_ids[None, :] < tile_count[:, None]) & (
        tile_cols // strip_count == half_index
    )
    position = jnp.cumsum(live_slots.astype(jnp.int32), axis=1) - 1
    chosen = live_slots[:, :, None] & (
        position[:, :, None] == jnp.arange(HS, dtype=jnp.int32)[None, None, :]
    )
    picked = jnp.einsum(
        "isq,isx->iqx",
        chosen.astype(jnp.bfloat16),
        tile_blocks,
        preferred_element_type=jnp.bfloat16,
    )
    inner_rows = jnp.sum(
        jnp.where(chosen, (tile_cols - half_index * strip_count)[:, :, None], 0), axis=1
    ).astype(jnp.int32)
    used_flags = jnp.any(chosen, axis=1).astype(jnp.int32)
    return (picked, inner_rows, used_flags)


def section_term(
    picked, inner_rows, used_flags, right_blocks, right_cols, right_count, out_cols, out_live
):
    strip_count = picked.shape[0]
    slot_count = out_cols.shape[1]
    gathered = right_blocks[inner_rows]
    gathered_cols = right_cols[inner_rows]
    gathered_count = right_count[inner_rows]
    slot_ids = jnp.arange(slot_count, dtype=jnp.int32)
    right_live = slot_ids[None, None, :] < gathered_count[:, :, None]
    matches = (gathered_cols[:, :, :, None] == out_cols[:, None, None, :]) & right_live[
        :, :, :, None
    ]
    matches = matches & (used_flags[:, :, None, None] > 0) & out_live[:, None, None, :]
    selected = jnp.einsum(
        "iqbj,iqbx->iqjx",
        matches.astype(jnp.bfloat16),
        gathered,
        preferred_element_type=jnp.bfloat16,
    )
    left_blocks = picked.reshape(strip_count, HS, BLK, BLK)
    right_sel = selected.reshape(strip_count, HS, slot_count, BLK, BLK)
    contribution = jnp.einsum(
        "iqmn,iqjnp->ijmp", left_blocks, right_sel, preferred_element_type=jnp.float32
    )
    return contribution.reshape(strip_count, slot_count, BLK * BLK)


def dense_local(blocks, columns, counts):
    count_now = counts[:, 0]
    strip_count = columns.shape[0]
    slot_count = columns.shape[1]
    out_live = jnp.arange(slot_count, dtype=jnp.int32)[None, :] < count_now[:, None]
    col_index = lax.axis_index("col")
    col_total = lax.axis_size("col")
    accumulated = jnp.zeros((strip_count, slot_count, blocks.shape[2]), jnp.float32)
    right_tile = (blocks, columns, count_now)
    for section in range(SECTIONS):
        target_piece = (col_index + section) % col_total
        root_index = target_piece // 2
        half_index = target_piece % 2
        got_blocks, got_cols, got_count = (
            broadcast(blocks, "row", root_index),
            broadcast(columns, "row", root_index),
            broadcast(count_now, "row", root_index),
        )
        picked, inner_rows, used_flags = compact(got_blocks, got_cols, got_count, half_index)
        if section > 0:
            right_tile = from_behind((right_tile[0], right_tile[1], right_tile[2]), "col", -1)
        accumulated = accumulated + section_term(
            picked,
            inner_rows,
            used_flags,
            right_tile[0],
            right_tile[1],
            right_tile[2],
            columns,
            out_live,
        )
    return accumulated.astype(jnp.bfloat16)


def columns_kernel(n_row, n_col, live, every, rs, rr, cs, cr):
    me, col = lax.axis_index("row"), lax.axis_index("col")
    barrier = pltpu.get_barrier_semaphore()

    def row_peer(step):
        return lax.rem(me + step, n_row), col

    def col_peer(step):
        return me, lax.rem(col + step, n_col)

    for step in range(1, n_row):
        pl.semaphore_signal(barrier, inc=1, device_id=row_peer(step), device_id_type=MESH)
    for step in range(1, n_col):
        pl.semaphore_signal(barrier, inc=1, device_id=col_peer(step), device_id_type=MESH)
    every[col * n_row + me] = live[...]
    pl.semaphore_wait(barrier, n_row + n_col - 2)

    def along_row(step, owner):
        return pltpu.make_async_remote_copy(
            src_ref=live, dst_ref=every.at[col * n_row + owner],
            send_sem=rs.at[step], recv_sem=rr.at[step],
            device_id=row_peer(step), device_id_type=MESH,
        )

    def along_col(step, owner):
        return pltpu.make_async_remote_copy(
            src_ref=every.at[pl.ds(col * n_row, n_row)],
            dst_ref=every.at[pl.ds(owner * n_row, n_row)],
            send_sem=cs.at[step], recv_sem=cr.at[step],
            device_id=col_peer(step), device_id_type=MESH,
        )

    for step in range(1, n_row):
        along_row(step, me).start()
    for step in range(1, n_row):
        along_row(step, lax.rem(me + n_row - step, n_row)).wait_recv()
    for step in range(1, n_col):
        along_col(step, col).start()
    for step in range(1, n_row):
        along_row(step, me).wait_send()
    for step in range(1, n_col):
        along_col(step, lax.rem(col + n_col - step, n_col)).wait_recv()
    for step in range(1, n_col):
        along_col(step, col).wait_send()


def match_kernel(n_row, n_col, rows, every, per_row, listed):
    slots, wide = every.shape[1:]
    combos = slots * slots
    me, col = lax.axis_index("row"), lax.axis_index("col")
    lane = lax.broadcasted_iota(jnp.int32, (combos, wide), 1)

    def found_in(c, section, q):
        piece = lax.rem(c + section, n_col)
        left = every[c * n_row + piece // 2]
        right = every[piece * n_row + q]
        out = every[c * n_row + q]
        left = jnp.concatenate(
            [jnp.broadcast_to(left[t : t + 1], (slots, wide)) for t in range(slots)], axis=0
        )
        out = jnp.where(lane < rows, jnp.concatenate([out] * slots, axis=0), -1)
        left = left - lax.rem(piece, 2) * rows
        inner = jnp.zeros((combos, wide), jnp.int32)
        reach = [jnp.full((combos, wide), -2, jnp.int32) for _ in range(slots)]
        for step in range(BAND):
            there = jnp.where(lane + step < rows, lane + step, lane + step - rows)
            hit = left == there
            inner = jnp.where(hit, there, inner)
            moved = right if step == 0 else pltpu.roll(right, wide - step, 1)
            for b in range(slots):
                reach[b] = jnp.where(
                    hit, jnp.broadcast_to(moved[b : b + 1], (combos, wide)), reach[b]
                )
        found = jnp.zeros((combos, wide), jnp.int32)
        which = jnp.zeros((combos, wide), jnp.int32)
        for b in range(slots):
            same = (reach[b] == out) & (out >= 0)
            found = jnp.where(same, 1, found)
            which = jnp.where(same, b, which)
        return found, inner, which

    group = SECTIONS * n_row

    def count(which, carry):
        c = which // group
        rest = which - c * group
        found, _, _ = found_in(c, rest // n_row, lax.rem(rest, n_row))
        per_row[which, 0:1] = jnp.sum(found, axis=0, keepdims=True)
        distinct = [
            jnp.max(found[t * slots : (t + 1) * slots], axis=0, keepdims=True)
            for t in range(slots)
        ]
        per_row[which, 1:2] = sum(distinct)
        return carry

    lax.fori_loop(0, n_col * group, count, 0)

    up_r = lax.broadcasted_iota(jnp.int32, (wide, wide), 0)
    up_c = lax.broadcasted_iota(jnp.int32, (wide, wide), 1)
    before_row = jnp.where(up_r < up_c, 1.0, 0.0).astype(jnp.bfloat16)
    in_r = lax.broadcasted_iota(jnp.int32, (combos, combos), 0)
    in_c = lax.broadcasted_iota(jnp.int32, (combos, combos), 1)
    before_combo = jnp.where(in_c < in_r, 1.0, 0.0).astype(jnp.bfloat16)
    high = lax.broadcasted_iota(jnp.int32, (HIGH, wide), 0)
    low = lax.broadcasted_iota(jnp.int32, (LOW, wide), 0)
    row = lax.broadcasted_iota(jnp.int32, (1, wide), 1).astype(jnp.float32)

    def build(which, carry):
        last = which == group
        c = jnp.where(last, lax.rem(col + n_col - 1, n_col), col)
        section = jnp.where(last, SECTIONS - 1, which // n_row)
        q = jnp.where(last, me, lax.rem(which, n_row))
        found, inner, slot = found_in(c, section, q)
        ones = found.astype(jnp.float32)
        base = jnp.dot(
            jnp.broadcast_to(jnp.sum(ones, axis=0, keepdims=True), (combos, wide)).astype(
                jnp.bfloat16
            ),
            before_row,
            preferred_element_type=jnp.float32,
        )
        inside = jnp.dot(
            before_combo, ones.astype(jnp.bfloat16), preferred_element_type=jnp.float32
        )
        place = jnp.where(found > 0, (base + inside).astype(jnp.int32), -1)
        total = jnp.zeros((3 * HIGH, LOW), jnp.float32)
        for combo in range(combos):
            at = place[combo : combo + 1]
            on = high == at // LOW
            small = (slot[combo : combo + 1] * combos + combo).astype(jnp.float32)
            deep = inner[combo : combo + 1].astype(jnp.float32)
            values = jnp.concatenate(
                [
                    jnp.where(on, jnp.broadcast_to(value, (HIGH, wide)), 0.0)
                    for value in (row, deep, small)
                ],
                axis=0,
            ).astype(jnp.bfloat16)
            keys = jnp.where((low == lax.rem(at, LOW)) & (at >= 0), 1.0, 0.0)
            total += lax.dot_general(
                values,
                keys.astype(jnp.bfloat16),
                (((1,), (1,)), ((), ())),
                preferred_element_type=jnp.float32,
            )
        listed[which] = total.astype(jnp.int32)
        return carry

    lax.fori_loop(0, group + 1, build, 0)


def gather_kernel(
    n_row, lists, spots, counts, tile, r_self, r_send, l_first, l_next, l_send
):
    me = lax.axis_index("row")
    col = lax.axis_index("col")
    n_col = lax.axis_size("col")

    def pick_right(which, dst):
        def some(step, carry):
            for part in range(UNROLL):
                k = step * UNROLL + part
                dst[k] = tile[lax.rem(lists[which, k] // SHIFT, SHIFT)]
            return carry

        lax.fori_loop(0, (counts[which] + UNROLL - 1) // UNROLL, some, 0)

    def pick_left(which, dst):
        def one(k, carry):
            dst[spots[which, k]] = tile[lax.rem(lists[which, k], SHIFT)]
            return carry

        lax.fori_loop(0, counts[which], one, 0)

    pick_right(me, r_self)
    pick_right(2 * n_row, r_send)
    for section, own in enumerate((l_first, l_next)):
        owner = lax.rem(col + section, n_col) // 2

        @pl.when(owner == me)
        def _():
            def one(q, carry):
                pick_left(section * n_row + q, l_send.at[section, q])
                return carry

            pick_left(section * n_row + me, own)
            lax.fori_loop(0, me, one, 0)
            lax.fori_loop(me + 1, n_row, one, 0)


def exchange_kernel(
    n_row, n_col, r_send, l_send, r_recv, l_recv, rs, rr, ls, lr
):
    me = lax.axis_index("row")
    col = lax.axis_index("col")
    ahead, behind = lax.rem(col + 1, n_col), lax.rem(col + n_col - 1, n_col)
    barrier = pltpu.get_barrier_semaphore()
    pl.semaphore_signal(barrier, inc=1, device_id=(me, ahead), device_id_type=MESH)
    pl.semaphore_signal(barrier, inc=1, device_id=(me, behind), device_id_type=MESH)
    for step in range(1, n_row):
        peer = lax.rem(me + step, n_row)
        pl.semaphore_signal(barrier, inc=1, device_id=(peer, col), device_id_type=MESH)
    pl.semaphore_wait(barrier, n_row + 1)

    right = pltpu.make_async_remote_copy(
        src_ref=r_send, dst_ref=r_recv, send_sem=rs, recv_sem=rr,
        device_id=(me, behind), device_id_type=MESH,
    )
    right.start()

    def left(section, step):
        peer = lax.rem(me + step, n_row)
        return pltpu.make_async_remote_copy(
            src_ref=l_send.at[section, peer], dst_ref=l_recv.at[section],
            send_sem=ls.at[section, step], recv_sem=lr.at[section],
            device_id=(peer, col), device_id_type=MESH,
        )

    owners = [lax.rem(col + section, n_col) // 2 for section in range(SECTIONS)]
    for section in range(SECTIONS):

        @pl.when(owners[section] == me)
        def _():
            for step in range(1, n_row):
                left(section, step).start()

    for section in range(SECTIONS):

        @pl.when(owners[section] == me)
        def _():
            for step in range(1, n_row):
                left(section, step).wait_send()

        @pl.when(owners[section] != me)
        def _():
            left(section, 1).wait_recv()

    right.wait()


def product_kernel(
    slots, lists, spots, counts, distinct, l_first, l_next, l_recv, r_self, r_recv,
    out, total, first, second, done,
):
    rows = out.shape[0]
    deep = BLK // 2
    wide = 2 * BLK
    tiles = BLK * BLK // wide
    spare = rows * slots

    def clear(i, carry):
        out[i] = jnp.zeros((slots, BLK * BLK), out.dtype)
        done[i] = 0
        return carry

    lax.fori_loop(0, rows, clear, 0)

    src = lax.broadcasted_iota(jnp.int32, (wide, wide), 0)
    dst = lax.broadcasted_iota(jnp.int32, (wide, wide), 1)
    place = (src // BLK) * BLK + (src % 2) * deep + (src % BLK) // 2
    order = jnp.where(place == dst, 1.0, 0.0).astype(jnp.bfloat16)
    lane = lax.broadcasted_iota(jnp.int32, (deep, wide), 1)

    me, col = lax.axis_index("row"), lax.axis_index("col")
    n_col = lax.axis_size("col")
    batch = 8

    def reorder(section, source, ready):
        def some(step, carry):
            here = pl.ds(step * batch, batch)
            ready[here] = (
                jnp.dot(
                    source[here].reshape(batch * deep, wide),
                    order,
                    preferred_element_type=jnp.float32,
                )
                .astype(jnp.bfloat16)
                .reshape(batch, deep, wide)
            )
            return carry

        lax.fori_loop(0, (distinct[section] + batch - 1) // batch, some, 0)

    for section, (own, ready) in enumerate(((l_first, first), (l_next, second))):
        owner = lax.rem(col + section, n_col) // 2

        @pl.when(owner == me)
        def _():
            reorder(section, own, ready)

        @pl.when(owner != me)
        def _():
            reorder(section, l_recv.at[section], ready)

        def start(k, carry):
            row = lax.rem(lists[section, k], SHIFT) // slots
            total[pl.ds(row * (slots * deep), slots * deep), :] = jnp.zeros(
                (slots * deep, wide), jnp.float32
            )
            return carry

        lax.fori_loop(0, counts[section], start, 0)

    for section, (ready, rights) in enumerate(((first, r_self), (second, r_recv))):
        count = counts[section]

        def multiply(step, carry):
            found = []
            for part in range(UNROLL):
                k = step * UNROLL + part
                block = rights[k].astype(jnp.float32)
                turned = pltpu.roll(block, BLK, 1)
                weight = jnp.concatenate(
                    [
                        jnp.where(lane < BLK, block, 0.0),
                        jnp.where(lane < BLK, turned, 0.0),
                        jnp.where(lane < BLK, 0.0, turned),
                        jnp.where(lane < BLK, 0.0, block),
                    ],
                    axis=0,
                ).astype(jnp.bfloat16)
                found.append(
                    jnp.dot(
                        ready[spots[section, k]],
                        weight,
                        preferred_element_type=jnp.float32,
                    )
                )
            for part in range(UNROLL):
                k = step * UNROLL + part
                code = lists[section, k]
                target = lax.rem(code, SHIFT) // slots * slots + code // (SHIFT * SHIFT)
                target = jnp.where(k < count, target, spare)
                total[pl.ds(target * deep, deep), :] += found[part]
            return carry

        lax.fori_loop(0, (count + UNROLL - 1) // UNROLL, multiply, 0)

    for section in range(SECTIONS):

        def finish(k, carry):
            row = lax.rem(lists[section, k], SHIFT) // slots

            @pl.when(done[row] == 0)
            def _():
                done[row] = 1
                for part in range(tiles):
                    piece = total[pl.ds(row * (slots * deep) + part, slots, stride=deep), :]
                    out[row, :, part * wide : (part + 1) * wide] = piece.astype(out.dtype)

            return carry

        lax.fori_loop(0, counts[section], finish, 0)


def sparse_local(blocks, lists, spots, counts, distinct):
    rows, slots, size = blocks.shape
    n_row, n_col = lax.axis_size("row"), lax.axis_size("col")
    me = lax.axis_index("row")
    form = (BLK // 2, 2 * BLK)
    tile = blocks.reshape((rows * slots,) + form)
    smem = pl.BlockSpec(memory_space=pltpu.SMEM)
    vmem = pl.BlockSpec(memory_space=pltpu.VMEM)
    anywhere = pl.BlockSpec(memory_space=pl.ANY)
    kept = jax.ShapeDtypeStruct((KEEP,) + form, jnp.bfloat16)
    sent = jax.ShapeDtypeStruct((SEND,) + form, jnp.bfloat16)
    left = (SECTIONS, n_row, LEFT) + form
    r_self, r_send, l_first, l_next, l_send = pl.pallas_call(
        functools.partial(gather_kernel, n_row),
        out_shape=(kept, sent, kept, sent, jax.ShapeDtypeStruct(left, jnp.bfloat16)),
        in_specs=[smem, smem, smem, vmem],
        out_specs=(vmem,) * 5,
        compiler_params=pltpu.CompilerParams(vmem_limit_bytes=VMEM_LIMIT),
        name="pick_blocks",
    )(lists, spots, counts, tile)
    r_recv, l_recv = pl.pallas_call(
        functools.partial(exchange_kernel, n_row, n_col),
        out_shape=(sent, jax.ShapeDtypeStruct(left[:1] + left[2:], jnp.bfloat16)),
        in_specs=[anywhere] * 2,
        out_specs=(anywhere,) * 2,
        scratch_shapes=[
            pltpu.SemaphoreType.DMA,
            pltpu.SemaphoreType.DMA,
            pltpu.SemaphoreType.DMA((SECTIONS, n_row)),
            pltpu.SemaphoreType.DMA((SECTIONS,)),
        ],
        compiler_params=pltpu.CompilerParams(collective_id=0, has_side_effects=True),
        name="exchange_blocks",
    )(r_send, l_send)
    mine = jnp.stack([me, n_row + me])
    return pl.pallas_call(
        functools.partial(product_kernel, slots),
        out_shape=jax.ShapeDtypeStruct(blocks.shape, jnp.bfloat16),
        in_specs=[smem] * 4 + [vmem] * 5,
        out_specs=vmem,
        scratch_shapes=[
            pltpu.VMEM(((rows * slots + 1) * form[0], form[1]), jnp.float32),
            pltpu.VMEM((KEEP,) + form, jnp.bfloat16),
            pltpu.VMEM((SEND,) + form, jnp.bfloat16),
            pltpu.SMEM((rows,), jnp.int32),
        ],
        compiler_params=pltpu.CompilerParams(vmem_limit_bytes=VMEM_LIMIT),
        name="multiply_blocks",
    )(
        lists[mine], spots[mine], counts[mine], distinct[mine],
        l_first, l_next, l_recv, r_self, r_recv,
    )


def local(blocks, columns, counts):
    rows, slots = columns.shape
    n_row, n_col = lax.axis_size("row"), lax.axis_size("col")
    me, col = lax.axis_index("row"), lax.axis_index("col")
    slot_ids = jnp.arange(slots, dtype=jnp.int32)
    live = jnp.where(slot_ids[None, :] < counts, columns, -1).T
    wide = -(-(rows + BAND) // 128) * 128
    fill = jnp.full((slots, wide - rows - BAND), -1, jnp.int32)
    live = jnp.concatenate([live, live[:, :BAND], fill], axis=1)
    vmem = pl.BlockSpec(memory_space=pltpu.VMEM)
    every = pl.pallas_call(
        functools.partial(columns_kernel, n_row, n_col),
        out_shape=jax.ShapeDtypeStruct((n_col * n_row, slots, wide), jnp.int32),
        in_specs=[vmem],
        out_specs=vmem,
        scratch_shapes=[
            pltpu.SemaphoreType.DMA((n_row,)),
            pltpu.SemaphoreType.DMA((n_row,)),
            pltpu.SemaphoreType.DMA((n_col,)),
            pltpu.SemaphoreType.DMA((n_col,)),
        ],
        compiler_params=pltpu.CompilerParams(collective_id=1, has_side_effects=True),
        name="exchange_columns",
    )(live)

    group = SECTIONS * n_row
    per_row, listed = pl.pallas_call(
        functools.partial(match_kernel, n_row, n_col, rows),
        out_shape=(
            jax.ShapeDtypeStruct((n_col * group, 2, wide), jnp.int32),
            jax.ShapeDtypeStruct((group + 1, 3 * HIGH, LOW), jnp.int32),
        ),
        in_specs=[vmem],
        out_specs=(vmem, vmem),
        compiler_params=pltpu.CompilerParams(vmem_limit_bytes=VMEM_LIMIT),
        name="match_columns",
    )(every)
    both = jnp.sum(per_row, axis=2).reshape(n_col, SECTIONS, n_row, 2)
    totals, distinct = both[..., 0], both[..., 1]
    c = jnp.arange(n_col)[:, None, None]
    s = jnp.arange(SECTIONS)[None, :, None]
    stays = jnp.arange(n_row)[None, None, :] == (c + s) % n_col // 2
    fits = jnp.all((totals <= jnp.where(s == 0, KEEP, SEND)) & (stays | (distinct <= LEFT)))

    behind = lax.rem(col + n_col - 1, n_col)

    def ours(array):
        first = lax.dynamic_index_in_dim(array, col, 0, keepdims=False).reshape(group)
        last = lax.dynamic_slice(array, (behind, SECTIONS - 1, me), (1, 1, 1)).reshape(1)
        return jnp.concatenate([first, last])

    sizes, distinct = ours(totals), ours(distinct)
    row, inner, small = [
        listed[:, part * HIGH : (part + 1) * HIGH].reshape(group + 1, HIGH * LOW)
        for part in range(3)
    ]
    slot = small // (slots * slots)
    combo = small % (slots * slots)
    lists = row * slots + combo // slots + SHIFT * (inner * slots + slot)
    lists = lists + SHIFT * SHIFT * (combo % slots)
    source = row * slots + combo // slots
    rank = jnp.arange(HIGH * LOW, dtype=jnp.int32)
    fresh = (source != jnp.roll(source, 1, axis=1)) | (rank == 0)
    fresh = (fresh & (rank < sizes[:, None])).astype(jnp.bfloat16)
    through = jnp.triu(jnp.ones((HIGH * LOW, HIGH * LOW), jnp.bfloat16))
    spots = jnp.dot(fresh, through, preferred_element_type=jnp.float32).astype(jnp.int32)
    spots = jnp.maximum(spots - 1, 0)
    return lax.cond(
        fits,
        lambda: sparse_local(blocks, lists, spots, sizes, distinct),
        lambda: dense_local(blocks, columns, counts),
    )


def solution(mesh):
    return jax.shard_map(
        local,
        mesh=mesh,
        in_specs=(P("col", "row", None), P("col", "row"), P("col", "row")),
        out_specs=P("col", "row", None),
        check_vma=False,
    )
```
